32 devices in a mesh: row: 4 (over y, x), col: 8 (over z, core).
Axes of the slice: x: 2, y: 2, z: 4, core: 2. Of those that a mesh axis runs over, the one named last changes fastest.
Arguments:
- amplitude: float32 [32, 80, 5, 640], P('col', 'row'), may hold values from -6 to 6
- coupling: float32 [80, 5, 32, 640], P('row', None, 'col'), may hold values from -0.3125 to 0.3125
Outputs:
- cycle_term: float32 [32, 640, 32, 640], P('row', None, 'col')
The draws below stay inside these ranges and needn't reach their ends.
All inputs are finite; a program needn't handle non-finite values.
Results may differ from the reference program's by a relative error of at most 0.00005.
Values sent between devices are 32-bit elements; how exact they have to be, the bound alone decides.
A program may use at most 192 MiB of HBM per device.

```python
import jax
import jax.numpy as jnp
from jax import lax

O = 80
V = 640
CB = 5
OW = 32


def levels(own_key, shape, split, low, high):
    def one(dim, blocks):
        steps = jax.random.uniform(jax.random.fold_in(jax.random.fold_in(own_key, 6), dim), (blocks,), jnp.float32, low / len(split), high / len(split))
        return jnp.repeat(jnp.exp(steps), shape[dim] // blocks).reshape((-1,) + (1,) * (len(shape) - dim - 1))

    factor_of = one(*split[0])
    for cut in split[1:]:
        factor_of = factor_of * one(*cut)
    return factor_of


def bell_draw(own_key, shape, width, bound, split=(), kind=jnp.bfloat16):
    level = levels(own_key, shape, split, -0.22, 0.18) if split else 1.0
    values = jax.random.normal(own_key, shape, jnp.float32) * width * level
    return jnp.minimum(jnp.maximum(values, -bound), bound).astype(kind)


def setup_inputs(seed: int = 0) -> dict:
    key_list = jax.random.split(jax.random.key(seed), 3)
    amplitude = bell_draw(key_list[0], (OW, O, CB, V), 1.0, 6.0, ((0, 8), (1, 4)), jnp.float32)
    coupling = bell_draw(key_list[1], (O, CB, OW, V), (O * CB) ** -0.5, 0.3125, ((0, 4), (2, 8)), jnp.float32)
    return dict(amplitude=amplitude, coupling=coupling)


def reference(amplitude, coupling):
    def one_row(index):
        own = lax.dynamic_index_in_dim(amplitude, index, 0, keepdims=False)
        side = lax.dynamic_index_in_dim(coupling, index, 2, keepdims=False)
        direct = jnp.einsum("kca,kcjb->ajb", own, coupling, precision=lax.Precision.HIGHEST)
        mirror = jnp.einsum("jkcb,kca->ajb", amplitude, side, precision=lax.Precision.HIGHEST)
        return direct + mirror

    return lax.map(one_row, jnp.arange(OW, dtype=jnp.int32))
```

```python
import functools

import jax
import jax.numpy as jnp
from jax import lax
from jax.experimental import pallas as pl
from jax.experimental.pallas import tpu as pltpu
from jax.sharding import PartitionSpec as P

MESH = pl.DeviceIdType.MESH


def gather_kernel(
    rows, parts, s_ref, right_ref, left_ref,
    own_sem, row_send, row_recv, up_send, down_send, chain_recv, side_send, side_recv, keep_sem,
):
    r = lax.axis_index("row")
    col = lax.axis_index("col")
    q = col // 2
    c = col % 2
    sibling = 2 * q + 1 - c
    above = lax.rem(col + 2, 2 * rows)
    below = lax.rem(col + 2 * rows - 2, 2 * rows)
    is_source = q == r
    goes_up = jnp.logical_and(q >= r, q < rows - 1)
    goes_down = jnp.logical_and(q <= r, q > 0)

    def origin(t):
        return lax.rem(r - t + rows, rows)

    barrier = pltpu.get_barrier_semaphore()
    for t in range(1, rows):
        pl.semaphore_signal(barrier, inc=1, device_id=(lax.rem(r + t, rows), col), device_id_type=MESH)
    for other in (above, below, sibling):
        pl.semaphore_signal(barrier, inc=1, device_id=(r, other), device_id_type=MESH)
    pl.semaphore_wait(barrier, rows + 2)

    def row_copy(t, p):
        return pltpu.make_async_remote_copy(
            src_ref=s_ref.at[p], dst_ref=right_ref.at[r, p],
            send_sem=row_send.at[t, p], recv_sem=row_recv.at[t, p],
            device_id=(lax.rem(r + t, rows), col), device_id_type=MESH,
        )

    def row_arrival(t, p):
        return pltpu.make_async_remote_copy(
            src_ref=s_ref.at[p], dst_ref=right_ref.at[origin(t), p],
            send_sem=row_send.at[t, p], recv_sem=row_recv.at[t, p],
            device_id=(lax.rem(r + t, rows), col), device_id_type=MESH,
        )

    def chain_copy(src, t, p, sem, target, arrival):
        return pltpu.make_async_remote_copy(
            src_ref=src, dst_ref=left_ref.at[c, origin(t), p],
            send_sem=sem.at[t, p], recv_sem=arrival.at[t, p],
            device_id=(r, target), device_id_type=MESH,
        )

    def side_arrival(t, p):
        return pltpu.make_async_remote_copy(
            src_ref=s_ref.at[p], dst_ref=left_ref.at[1 - c, origin(t), p],
            send_sem=side_send.at[t, p], recv_sem=side_recv.at[t, p],
            device_id=(r, sibling), device_id_type=MESH,
        )

    def keep_copy(src, t, p):
        return pltpu.make_async_copy(src, left_ref.at[c, origin(t), p], keep_sem.at[t, p])

    def forward(src, t, p):
        @pl.when(goes_up)
        def _():
            chain_copy(src, t, p, up_send, above, chain_recv).start()

        @pl.when(goes_down)
        def _():
            chain_copy(src, t, p, down_send, below, chain_recv).start()

        chain_copy(src, t, p, side_send, sibling, side_recv).start()

    def step(t, p, first):
        @pl.when(is_source)
        def _():
            if first:
                src = s_ref.at[p]
            else:
                row_arrival(t, p).wait_recv()
                src = right_ref.at[origin(t), p]
            forward(src, t, p)
            keep_copy(src, t, p).start()

        @pl.when(jnp.logical_not(is_source))
        def _():
            src = left_ref.at[c, origin(t), p]
            chain_copy(src, t, p, up_send, above, chain_recv).wait_recv()
            forward(src, t, p)

    own = pltpu.make_async_copy(s_ref, right_ref.at[r], own_sem)
    own.start()

    def send_rows(p, carry):
        for t in range(1, rows):
            row_copy(t, p).start()
        return carry

    lax.fori_loop(0, parts, send_rows, 0)

    def first_step(p, carry):
        step(0, p, True)
        return carry

    lax.fori_loop(0, parts, first_step, 0)

    def later_step(n, carry):
        step(1 + lax.rem(n, rows - 1), n // (rows - 1), False)
        return carry

    lax.fori_loop(0, parts * (rows - 1), later_step, 0)

    own.wait()

    def finish_rows(n, carry):
        t = 1 + lax.rem(n, rows - 1)
        p = n // (rows - 1)
        row_copy(t, p).wait_send()

        @pl.when(jnp.logical_not(is_source))
        def _():
            row_arrival(t, p).wait_recv()

        return carry

    lax.fori_loop(0, parts * (rows - 1), finish_rows, 0)

    def finish_chain(n, carry):
        t = lax.rem(n, rows)
        p = n // rows
        src = s_ref.at[p]

        @pl.when(goes_up)
        def _():
            chain_copy(src, t, p, up_send, above, chain_recv).wait_send()

        @pl.when(goes_down)
        def _():
            chain_copy(src, t, p, down_send, below, chain_recv).wait_send()

        chain_copy(src, t, p, side_send, sibling, side_recv).wait_send()
        side_arrival(t, p).wait_recv()

        @pl.when(is_source)
        def _():
            keep_copy(src, t, p).wait()

        return carry

    lax.fori_loop(0, parts * rows, finish_chain, 0)


def gather(s, rows):
    parts, depth, width = s.shape
    sems = pltpu.SemaphoreType.DMA((rows, parts))
    return pl.pallas_call(
        functools.partial(gather_kernel, rows, parts),
        out_shape=(
            jax.ShapeDtypeStruct((rows, parts, depth, width), s.dtype),
            jax.ShapeDtypeStruct((2, rows, parts, depth, width), s.dtype),
        ),
        in_specs=[pl.BlockSpec(memory_space=pl.ANY)],
        out_specs=[pl.BlockSpec(memory_space=pl.ANY)] * 2,
        scratch_shapes=[pltpu.SemaphoreType.DMA] + [sems] * 8,
        compiler_params=pltpu.CompilerParams(collective_id=0, has_side_effects=True),
    )(s)


def split(x):
    high = x.astype(jnp.bfloat16)
    low = (x - high.astype(jnp.float32)).astype(jnp.bfloat16)
    return high, low


def product_kernel(rows, parts, depth, width, right_ref, left_ref, out_ref, flat, rhs, lhs):
    total = rows * depth
    body = total // 128 * 128
    rest = total - body
    padded = rhs.shape[0]
    half = depth // 2

    @pl.when(pl.program_id(0) == 0)
    def _():
        if padded > 3 * total:
            rhs[3 * total :, :] = jnp.zeros((padded - 3 * total, parts * width), jnp.bfloat16)
        for j in range(parts):
            for k in range(rows):
                flat[k * depth : k * depth + half, :] = right_ref[k, j, half:, :]
                flat[k * depth + half : (k + 1) * depth, :] = right_ref[k, j, :half, :]
            high, low = split(flat[...])
            cols = slice(j * width, (j + 1) * width)
            rhs[:body, cols] = high[:body]
            rhs[body : 2 * body, cols] = high[:body]
            rhs[2 * body : 3 * body, cols] = low[:body]
            if rest:
                base = 3 * body
                rhs[base : base + rest, cols] = high[body:]
                rhs[base + rest : base + 2 * rest, cols] = high[body:]
                rhs[base + 2 * rest : base + 3 * rest, cols] = low[body:]

    for k in range(rows):
        flat[k * depth : (k + 1) * depth, :] = left_ref[0, k, 0]
    for at in range(0, body, 128):
        high, low = split(flat[at : at + 128, :].T)
        lhs[:, at : at + 128] = high
        lhs[:, body + at : body + at + 128] = low
        lhs[:, 2 * body + at : 2 * body + at + 128] = high
    if rest:
        x = flat[body:, :]
        high = x.astype(jnp.bfloat16).astype(jnp.float32)
        pieces = [high, x - high, high]
        if padded > 3 * total:
            pieces.append(jnp.zeros((padded - 3 * total, width), jnp.float32))
        lhs[:, 3 * body :] = jnp.concatenate(pieces, axis=0).T.astype(jnp.bfloat16)

    blocks = width // 128
    for n in range(0, parts * blocks, 2):
        result = jnp.dot(lhs[...], rhs[:, n * 128 : (n + 2) * 128], preferred_element_type=jnp.float32)
        for h in range(2):
            j, b = divmod(n + h, blocks)
            out_ref[0, :, j, b * 128 : (b + 1) * 128] = result[:, h * 128 : (h + 1) * 128]


def product(right, left):
    rows, parts, depth, width = right.shape
    total = rows * depth
    padded = -(-3 * total // 128) * 128
    own_rows = 2 * parts
    return pl.pallas_call(
        functools.partial(product_kernel, rows, parts, depth, width),
        grid=(own_rows,),
        out_shape=jax.ShapeDtypeStruct((own_rows, width, parts, width), jnp.float32),
        in_specs=[
            pl.BlockSpec((rows, parts, depth, width), lambda i: (0, 0, 0, 0), pipeline_mode=pl.Buffered(1)),
            pl.BlockSpec((1, rows, 1, depth, width), lambda i: (i // parts, 0, i % parts, 0, 0)),
        ],
        out_specs=pl.BlockSpec((1, width, parts, width), lambda i: (i, 0, 0, 0)),
        scratch_shapes=[
            pltpu.VMEM((total, width), jnp.float32),
            pltpu.VMEM((padded, parts * width), jnp.bfloat16),
            pltpu.VMEM((width, padded), jnp.bfloat16),
        ],
        compiler_params=pltpu.CompilerParams(vmem_limit_bytes=58 * 1024 * 1024),
        cost_estimate=pl.CostEstimate(
            flops=2 * padded * own_rows * width * parts * width,
            bytes_accessed=4 * own_rows * width * parts * width,
            transcendentals=0,
        ),
    )(right, left)


def solution(mesh):
    rows = mesh.shape["row"]

    def shards(amplitude, coupling):
        parts, occupied, block, width = amplitude.shape
        depth = occupied * block
        mine = jnp.concatenate(
            [
                amplitude.reshape(parts, depth, width),
                jnp.transpose(coupling.reshape(depth, parts, width), (1, 0, 2)),
            ],
            axis=1,
        )
        right, left = gather(mine, rows)
        return product(right, left)

    placed = (P("col", "row", None, None), P("row", None, "col", None))
    return jax.shard_map(
        shards, mesh=mesh, in_specs=placed, out_specs=P("row", None, "col", None), check_vma=False
    )
```

```python
import functools

import jax
import jax.numpy as jnp
from jax import lax
from jax.experimental import pallas as pl
from jax.experimental.pallas import tpu as pltpu
from jax.sharding import PartitionSpec as P

MESH = pl.DeviceIdType.MESH


def gather_kernel(
    rows, parts, s_ref, right_ref, left_ref,
    own_sem, row_send, row_recv, up_send, down_send, chain_recv, side_send, side_recv,
):
    r = lax.axis_index("row")
    col = lax.axis_index("col")
    q = col // 2
    c = col % 2
    sibling = 2 * q + 1 - c
    above = lax.rem(col + 2, 2 * rows)
    below = lax.rem(col + 2 * rows - 2, 2 * rows)
    is_source = q == r
    goes_up = jnp.logical_and(q >= r, q < rows - 1)
    goes_down = jnp.logical_and(q <= r, q > 0)

    def origin(t):
        return lax.rem(r - t + rows, rows)

    barrier = pltpu.get_barrier_semaphore()
    for t in range(1, rows):
        pl.semaphore_signal(barrier, inc=1, device_id=(lax.rem(r + t, rows), col), device_id_type=MESH)
    for other in (above, below, sibling):
        pl.semaphore_signal(barrier, inc=1, device_id=(r, other), device_id_type=MESH)
    pl.semaphore_wait(barrier, rows + 2)

    def row_copy(t, p):
        return pltpu.make_async_remote_copy(
            src_ref=s_ref.at[p], dst_ref=right_ref.at[r, p],
            send_sem=row_send.at[t, p], recv_sem=row_recv.at[t, p],
            device_id=(lax.rem(r + t, rows), col), device_id_type=MESH,
        )

    def row_arrival(t, p):
        return pltpu.make_async_remote_copy(
            src_ref=s_ref.at[p], dst_ref=right_ref.at[origin(t), p],
            send_sem=row_send.at[t, p], recv_sem=row_recv.at[t, p],
            device_id=(lax.rem(r + t, rows), col), device_id_type=MESH,
        )

    def chain_copy(src, t, p, sem, target, arrival):
        return pltpu.make_async_remote_copy(
            src_ref=src, dst_ref=left_ref.at[c, origin(t), p],
            send_sem=sem.at[t, p], recv_sem=arrival.at[t, p],
            device_id=(r, target), device_id_type=MESH,
        )

    def side_arrival(t, p):
        return pltpu.make_async_remote_copy(
            src_ref=s_ref.at[p], dst_ref=left_ref.at[1 - c, origin(t), p],
            send_sem=side_send.at[t, p], recv_sem=side_recv.at[t, p],
            device_id=(r, sibling), device_id_type=MESH,
        )

    def forward(src, t, p):
        @pl.when(goes_up)
        def _():
            chain_copy(src, t, p, up_send, above, chain_recv).start()

        @pl.when(goes_down)
        def _():
            chain_copy(src, t, p, down_send, below, chain_recv).start()

        chain_copy(src, t, p, side_send, sibling, side_recv).start()

    def step(t, p, first):
        @pl.when(is_source)
        def _():
            if first:
                src = s_ref.at[p]
            else:
                row_arrival(t, p).wait_recv()
                src = right_ref.at[origin(t), p]
            forward(src, t, p)

        @pl.when(jnp.logical_not(is_source))
        def _():
            src = left_ref.at[c, origin(t), p]
            chain_copy(src, t, p, up_send, above, chain_recv).wait_recv()
            forward(src, t, p)

    own = pltpu.make_async_copy(s_ref, right_ref.at[r], own_sem)
    own.start()

    def send_rows(p, carry):
        for t in range(1, rows):
            row_copy(t, p).start()
        return carry

    lax.fori_loop(0, parts, send_rows, 0)

    def first_step(p, carry):
        step(0, p, True)
        return carry

    lax.fori_loop(0, parts, first_step, 0)

    def later_step(n, carry):
        step(1 + lax.rem(n, rows - 1), n // (rows - 1), False)
        return carry

    lax.fori_loop(0, parts * (rows - 1), later_step, 0)

    own.wait()

    def finish_rows(n, carry):
        t = 1 + lax.rem(n, rows - 1)
        p = n // (rows - 1)
        row_copy(t, p).wait_send()

        @pl.when(jnp.logical_not(is_source))
        def _():
            row_arrival(t, p).wait_recv()

        return carry

    lax.fori_loop(0, parts * (rows - 1), finish_rows, 0)

    def finish_chain(n, carry):
        t = lax.rem(n, rows)
        p = n // rows
        src = s_ref.at[p]

        @pl.when(goes_up)
        def _():
            chain_copy(src, t, p, up_send, above, chain_recv).wait_send()

        @pl.when(goes_down)
        def _():
            chain_copy(src, t, p, down_send, below, chain_recv).wait_send()

        chain_copy(src, t, p, side_send, sibling, side_recv).wait_send()
        side_arrival(t, p).wait_recv()
        return carry

    lax.fori_loop(0, parts * rows, finish_chain, 0)


def gather(s, rows):
    parts, depth, width = s.shape
    sems = pltpu.SemaphoreType.DMA((rows, parts))
    return pl.pallas_call(
        functools.partial(gather_kernel, rows, parts),
        out_shape=(
            jax.ShapeDtypeStruct((rows, parts, depth, width), s.dtype),
            jax.ShapeDtypeStruct((2, rows, parts, depth, width), s.dtype),
        ),
        in_specs=[pl.BlockSpec(memory_space=pl.ANY)],
        out_specs=[pl.BlockSpec(memory_space=pl.ANY)] * 2,
        scratch_shapes=[pltpu.SemaphoreType.DMA] + [sems] * 7,
        compiler_params=pltpu.CompilerParams(collective_id=0, has_side_effects=True),
    )(s)


def split(x):
    high = x.astype(jnp.bfloat16)
    low = (x - high.astype(jnp.float32)).astype(jnp.bfloat16)
    return high, low


def product_kernel(rows, parts, depth, width, right_ref, left_ref, out_ref, flat, rhs, even, odd):
    total = rows * depth
    body = total // 128 * 128
    rest = total - body
    padded = rhs.shape[0]
    half = depth // 2
    step = pl.program_id(0)
    q = lax.axis_index("col") // 2
    c = lax.axis_index("col") % 2

    def prepare_right():
        if padded > 3 * total:
            rhs[3 * total :, :] = jnp.zeros((padded - 3 * total, parts * width), jnp.bfloat16)
        for j in range(parts):
            for k in range(rows):
                flat[k * depth : k * depth + half, :] = right_ref[k, j, half:, :]
                flat[k * depth + half : (k + 1) * depth, :] = right_ref[k, j, :half, :]
            high, low = split(flat[...])
            cols = slice(j * width, (j + 1) * width)
            rhs[:body, cols] = high[:body]
            rhs[body : 2 * body, cols] = high[:body]
            rhs[2 * body : 3 * body, cols] = low[:body]
            if rest:
                base = 3 * body
                rhs[base : base + rest, cols] = high[body:]
                rhs[base + rest : base + 2 * rest, cols] = high[body:]
                rhs[base + 2 * rest : base + 3 * rest, cols] = low[body:]

    def prepare_chunk(lhs, at):
        if at < body:
            high, low = split(flat[at : at + 128, :].T)
            lhs[:, at : at + 128] = high
            lhs[:, body + at : body + at + 128] = low
            lhs[:, 2 * body + at : 2 * body + at + 128] = high
        elif rest:
            x = flat[body:, :]
            high = x.astype(jnp.bfloat16).astype(jnp.float32)
            pieces = [high, x - high, high]
            if padded > 3 * total:
                pieces.append(jnp.zeros((padded - 3 * total, width), jnp.float32))
            lhs[:, 3 * body :] = jnp.concatenate(pieces, axis=0).T.astype(jnp.bfloat16)

    chunks = list(range(0, body + 1, 128))
    blocks = width // 128

    def multiply(lhs, following):
        pending = list(chunks)
        for n in range(0, parts * blocks, 2):
            result = jnp.dot(lhs[...], rhs[:, n * 128 : (n + 2) * 128], preferred_element_type=jnp.float32)
            take = -(-len(chunks) * 2 // (parts * blocks))
            for at in pending[:take]:
                prepare_chunk(following, at)
            pending = pending[take:]
            for h in range(2):
                j, b = divmod(n + h, blocks)
                out_ref[0, :, j, b * 128 : (b + 1) * 128] = result[:, h * 128 : (h + 1) * 128]
        for at in pending:
            prepare_chunk(following, at)

    @pl.when(step == 0)
    def _():
        prepare_right()

    index = jnp.minimum(step, 2 * parts - 1)
    from_right = jnp.logical_and(q == lax.axis_index("row"), index // parts == c)

    @pl.when(from_right)
    def _():
        for k in range(rows):
            flat[k * depth : (k + 1) * depth, :] = right_ref[k, lax.rem(index, parts)]

    @pl.when(jnp.logical_not(from_right))
    def _():
        for k in range(rows):
            flat[k * depth : (k + 1) * depth, :] = left_ref[0, k, 0]

    @pl.when(step == 0)
    def _():
        for at in chunks:
            prepare_chunk(even, at)

    @pl.when(step % 2 == 1)
    def _():
        multiply(even, odd)

    @pl.when(jnp.logical_and(step % 2 == 0, step > 0))
    def _():
        multiply(odd, even)


def product(right, left):
    rows, parts, depth, width = right.shape
    total = rows * depth
    padded = -(-3 * total // 128) * 128
    own_rows = 2 * parts

    def left_block(step):
        i = jnp.minimum(step, own_rows - 1)
        return i // parts, 0, i % parts, 0, 0

    return pl.pallas_call(
        functools.partial(product_kernel, rows, parts, depth, width),
        grid=(own_rows + 1,),
        out_shape=jax.ShapeDtypeStruct((own_rows, width, parts, width), jnp.float32),
        in_specs=[
            pl.BlockSpec((rows, parts, depth, width), lambda i: (0, 0, 0, 0), pipeline_mode=pl.Buffered(1)),
            pl.BlockSpec((1, rows, 1, depth, width), left_block),
        ],
        out_specs=pl.BlockSpec((1, width, parts, width), lambda i: (jnp.maximum(i - 1, 0), 0, 0, 0)),
        scratch_shapes=[
            pltpu.VMEM((total, width), jnp.float32),
            pltpu.VMEM((padded, parts * width), jnp.bfloat16),
            pltpu.VMEM((width, padded), jnp.bfloat16),
            pltpu.VMEM((width, padded), jnp.bfloat16),
        ],
        compiler_params=pltpu.CompilerParams(vmem_limit_bytes=58 * 1024 * 1024),
        cost_estimate=pl.CostEstimate(
            flops=2 * padded * own_rows * width * parts * width,
            bytes_accessed=4 * own_rows * width * parts * width,
            transcendentals=0,
        ),
    )(right, left)


def solution(mesh):
    rows = mesh.shape["row"]

    def shards(amplitude, coupling):
        parts, occupied, block, width = amplitude.shape
        depth = occupied * block
        mine = jnp.concatenate(
            [
                amplitude.reshape(parts, depth, width),
                jnp.transpose(coupling.reshape(depth, parts, width), (1, 0, 2)),
            ],
            axis=1,
        )
        right, left = gather(mine, rows)
        return product(right, left)

    placed = (P("col", "row", None, None), P("row", None, "col", None))
    return jax.shard_map(
        shards, mesh=mesh, in_specs=placed, out_specs=P("row", None, "col", None), check_vma=False
    )
```

```python
import functools

import jax
import jax.numpy as jnp
from jax import lax
from jax.experimental import pallas as pl
from jax.experimental.pallas import tpu as pltpu
from jax.sharding import PartitionSpec as P

MESH = pl.DeviceIdType.MESH


def gather_kernel(
    rows, parts, s_ref, right_ref, left_ref,
    own_sem, row_send, row_recv, up_send, down_send, chain_recv, side_send, side_recv,
):
    r = lax.axis_index("row")
    col = lax.axis_index("col")
    q = col // 2
    c = col % 2
    sibling = 2 * q + 1 - c
    above = lax.rem(col + 2, 2 * rows)
    below = lax.rem(col + 2 * rows - 2, 2 * rows)
    is_source = q == r
    goes_up = jnp.logical_and(q >= r, q < rows - 1)
    goes_down = jnp.logical_and(q <= r, q > 0)

    def origin(t):
        return lax.rem(r - t + rows, rows)

    barrier = pltpu.get_barrier_semaphore()
    for t in range(1, rows):
        pl.semaphore_signal(barrier, inc=1, device_id=(lax.rem(r + t, rows), col), device_id_type=MESH)
    for other in (above, below, sibling):
        pl.semaphore_signal(barrier, inc=1, device_id=(r, other), device_id_type=MESH)
    pl.semaphore_wait(barrier, rows + 2)

    def row_copy(t, p):
        return pltpu.make_async_remote_copy(
            src_ref=s_ref.at[p], dst_ref=right_ref.at[r, p],
            send_sem=row_send.at[t, p], recv_sem=row_recv.at[t, p],
            device_id=(lax.rem(r + t, rows), col), device_id_type=MESH,
        )

    def row_arrival(t, p):
        return pltpu.make_async_remote_copy(
            src_ref=s_ref.at[p], dst_ref=right_ref.at[origin(t), p],
            send_sem=row_send.at[t, p], recv_sem=row_recv.at[t, p],
            device_id=(lax.rem(r + t, rows), col), device_id_type=MESH,
        )

    def chain_copy(src, t, p, sem, target, arrival):
        return pltpu.make_async_remote_copy(
            src_ref=src, dst_ref=left_ref.at[c, origin(t), p],
            send_sem=sem.at[t, p], recv_sem=arrival.at[t, p],
            device_id=(r, target), device_id_type=MESH,
        )

    def side_arrival(t, p):
        return pltpu.make_async_remote_copy(
            src_ref=s_ref.at[p], dst_ref=left_ref.at[1 - c, origin(t), p],
            send_sem=side_send.at[t, p], recv_sem=side_recv.at[t, p],
            device_id=(r, sibling), device_id_type=MESH,
        )

    def forward(src, t, p):
        @pl.when(goes_up)
        def _():
            chain_copy(src, t, p, up_send, above, chain_recv).start()

        @pl.when(goes_down)
        def _():
            chain_copy(src, t, p, down_send, below, chain_recv).start()

        chain_copy(src, t, p, side_send, sibling, side_recv).start()

    def step(t, p, first):
        @pl.when(is_source)
        def _():
            if first:
                src = s_ref.at[p]
            else:
                row_arrival(t, p).wait_recv()
                src = right_ref.at[origin(t), p]
            forward(src, t, p)

        @pl.when(jnp.logical_not(is_source))
        def _():
            src = left_ref.at[c, origin(t), p]
            chain_copy(src, t, p, up_send, above, chain_recv).wait_recv()
            forward(src, t, p)

    own = pltpu.make_async_copy(s_ref, right_ref.at[r], own_sem)
    own.start()

    def send_rows(p, carry):
        for t in range(1, rows):
            row_copy(t, p).start()
        return carry

    lax.fori_loop(0, parts, send_rows, 0)

    def first_step(p, carry):
        step(0, p, True)
        return carry

    lax.fori_loop(0, parts, first_step, 0)

    def later_step(n, carry):
        step(1 + lax.rem(n, rows - 1), n // (rows - 1), False)
        return carry

    lax.fori_loop(0, parts * (rows - 1), later_step, 0)

    own.wait()

    def finish_rows(n, carry):
        t = 1 + lax.rem(n, rows - 1)
        p = n // (rows - 1)
        row_copy(t, p).wait_send()

        @pl.when(jnp.logical_not(is_source))
        def _():
            row_arrival(t, p).wait_recv()

        return carry

    lax.fori_loop(0, parts * (rows - 1), finish_rows, 0)

    def finish_chain(n, carry):
        t = lax.rem(n, rows)
        p = n // rows
        src = s_ref.at[p]

        @pl.when(goes_up)
        def _():
            chain_copy(src, t, p, up_send, above, chain_recv).wait_send()

        @pl.when(goes_down)
        def _():
            chain_copy(src, t, p, down_send, below, chain_recv).wait_send()

        chain_copy(src, t, p, side_send, sibling, side_recv).wait_send()
        side_arrival(t, p).wait_recv()
        return carry

    lax.fori_loop(0, parts * rows, finish_chain, 0)


def gather(s, rows):
    parts, depth, width = s.shape
    sems = pltpu.SemaphoreType.DMA((rows, parts))
    return pl.pallas_call(
        functools.partial(gather_kernel, rows, parts),
        out_shape=(
            jax.ShapeDtypeStruct((rows, parts, depth, width), s.dtype),
            jax.ShapeDtypeStruct((2, rows, parts, depth, width), s.dtype),
        ),
        in_specs=[pl.BlockSpec(memory_space=pl.ANY)],
        out_specs=[pl.BlockSpec(memory_space=pl.ANY)] * 2,
        scratch_shapes=[pltpu.SemaphoreType.DMA] + [sems] * 7,
        compiler_params=pltpu.CompilerParams(collective_id=0, has_side_effects=True),
    )(s)


def split(x):
    high = x.astype(jnp.bfloat16)
    low = (x - high.astype(jnp.float32)).astype(jnp.bfloat16)
    return high, low


def product_kernel(rows, parts, depth, width, right_ref, left_ref, out_ref, flat, rhs, even, odd, woven):
    total = rows * depth
    body = total // 128 * 128
    rest = total - body
    padded = rhs.shape[0]
    half = depth // 2
    blocks = width // 128
    step = pl.program_id(0)
    q = lax.axis_index("col") // 2
    c = lax.axis_index("col") % 2

    def prepare_right():
        if padded > 3 * total:
            rhs[3 * total :, :] = jnp.zeros((padded - 3 * total, parts * width), jnp.bfloat16)
        for j in range(parts):
            for k in range(rows):
                flat[k * depth : k * depth + half, :] = right_ref[k, j, half:, :]
                flat[k * depth + half : (k + 1) * depth, :] = right_ref[k, j, :half, :]
            high, low = split(flat[...])
            for b in range(blocks):
                piece = slice(b * 128, (b + 1) * 128)
                cols = slice((b * parts + j) * 128, (b * parts + j + 1) * 128)
                rhs[:body, cols] = high[:body, piece]
                rhs[body : 2 * body, cols] = high[:body, piece]
                rhs[2 * body : 3 * body, cols] = low[:body, piece]
                if rest:
                    base = 3 * body
                    rhs[base : base + rest, cols] = high[body:, piece]
                    rhs[base + rest : base + 2 * rest, cols] = high[body:, piece]
                    rhs[base + 2 * rest : base + 3 * rest, cols] = low[body:, piece]

    def prepare_chunk(lhs, at):
        if at < body:
            high, low = split(flat[at : at + 128, :].T)
            lhs[:, at : at + 128] = high
            lhs[:, body + at : body + at + 128] = low
            lhs[:, 2 * body + at : 2 * body + at + 128] = high
        elif rest:
            x = flat[body:, :]
            high = x.astype(jnp.bfloat16).astype(jnp.float32)
            pieces = [high, x - high, high]
            if padded > 3 * total:
                pieces.append(jnp.zeros((padded - 3 * total, width), jnp.float32))
            lhs[:, 3 * body :] = jnp.concatenate(pieces, axis=0).T.astype(jnp.bfloat16)

    chunks = list(range(0, body + 1, 128))

    def multiply(lhs, following):
        pending = list(chunks)
        take = -(-len(chunks) // blocks)
        for b in range(blocks):
            mixed = woven.at[b % 2]
            for n in range(0, parts, 2):
                at = (b * parts + n) * 128
                result = jnp.dot(lhs[...], rhs[:, at : at + 256], preferred_element_type=jnp.float32)
                for h in range(2):
                    mixed[pl.ds(n + h, width, stride=parts), :] = result[:, h * 128 : (h + 1) * 128]
            for at in pending[:take]:
                prepare_chunk(following, at)
            pending = pending[take:]
            out_ref[0, :, :, b * 128 : (b + 1) * 128] = mixed[...].reshape(width, parts, 128)

    @pl.when(step == 0)
    def _():
        prepare_right()

    index = jnp.minimum(step, 2 * parts - 1)
    from_right = jnp.logical_and(q == lax.axis_index("row"), index // parts == c)

    @pl.when(from_right)
    def _():
        for k in range(rows):
            flat[k * depth : (k + 1) * depth, :] = right_ref[k, lax.rem(index, parts)]

    @pl.when(jnp.logical_not(from_right))
    def _():
        for k in range(rows):
            flat[k * depth : (k + 1) * depth, :] = left_ref[0, k, 0]

    @pl.when(step == 0)
    def _():
        for at in chunks:
            prepare_chunk(even, at)

    @pl.when(step % 2 == 1)
    def _():
        multiply(even, odd)

    @pl.when(jnp.logical_and(step % 2 == 0, step > 0))
    def _():
        multiply(odd, even)


def product(right, left):
    rows, parts, depth, width = right.shape
    total = rows * depth
    padded = -(-3 * total // 128) * 128
    own_rows = 2 * parts

    def left_block(step):
        i = jnp.minimum(step, own_rows - 1)
        return i // parts, 0, i % parts, 0, 0

    return pl.pallas_call(
        functools.partial(product_kernel, rows, parts, depth, width),
        grid=(own_rows + 1,),
        out_shape=jax.ShapeDtypeStruct((own_rows, width, parts, width), jnp.float32),
        in_specs=[
            pl.BlockSpec((rows, parts, depth, width), lambda i: (0, 0, 0, 0), pipeline_mode=pl.Buffered(1)),
            pl.BlockSpec((1, rows, 1, depth, width), left_block),
        ],
        out_specs=pl.BlockSpec((1, width, parts, width), lambda i: (jnp.maximum(i - 1, 0), 0, 0, 0)),
        scratch_shapes=[
            pltpu.VMEM((total, width), jnp.float32),
            pltpu.VMEM((padded, parts * width), jnp.bfloat16),
            pltpu.VMEM((width, padded), jnp.bfloat16),
            pltpu.VMEM((width, padded), jnp.bfloat16),
            pltpu.VMEM((2, width * parts, 128), jnp.float32),
        ],
        compiler_params=pltpu.CompilerParams(vmem_limit_bytes=58 * 1024 * 1024),
        cost_estimate=pl.CostEstimate(
            flops=2 * padded * own_rows * width * parts * width,
            bytes_accessed=4 * own_rows * width * parts * width,
            transcendentals=0,
        ),
    )(right, left)


def solution(mesh):
    rows = mesh.shape["row"]

    def shards(amplitude, coupling):
        parts, occupied, block, width = amplitude.shape
        depth = occupied * block
        mine = jnp.concatenate(
            [
                amplitude.reshape(parts, depth, width),
                jnp.transpose(coupling.reshape(depth, parts, width), (1, 0, 2)),
            ],
            axis=1,
        )
        right, left = gather(mine, rows)
        return product(right, left)

    placed = (P("col", "row", None, None), P("row", None, "col", None))
    return jax.shard_map(
        shards, mesh=mesh, in_specs=placed, out_specs=P("row", None, "col", None), check_vma=False
    )
```
